256 devices in a mesh: row: 8 (over x, core), col: 32 (over z, y).
Axes of the slice: x: 4, y: 4, z: 8, core: 2. Of those that a mesh axis runs over, the one named last changes fastest.
Arguments:
- source_coords: bfloat16 [32, 524288], P(None, 'row'), may hold values from -6 to 6
- target_coords: bfloat16 [32, 65536], P(None, 'col'), may hold values from -6 to 6
- source_order: int32 [8, 65536], P('row'), may hold values from 0 to 65535, each once within a row
- target_order: int32 [32, 2048], P('col'), may hold values from 0 to 2047, each once within a row
- source_mass: float32 [524288], P('row'), may hold values from -12 to 240
- target_mass: float32 [65536], P('col'), may hold values from -12 to -8
- target_potential: float32 [65536], P('col'), may hold values from -4 to 24
- tile_source: int32 [8, 32, 256], P('row', 'col'), may hold values from 0 to 255, as said below
- tile_target: int32 [8, 32, 256], P('row', 'col'), may hold values from 0 to 7, as said below
- tile_count: int32 [8, 32], P('row', 'col'), may hold values from 64 to 256, as said below
Outputs:
- source_update: float32 [524288], P('row')
- target_update: float32 [65536], P('col')
The draws below stay inside these ranges and needn't reach their ends.
Inputs may be any that keep to these rules, and one draw needn't show every extreme that they name: Entries k < tile_count[r, c] of an intersection are used; later entries hold valid block numbers and are not part of the support. Within the used entries of an intersection no pair (tile_source, tile_target) repeats. Every source block of a row cluster has a used entry in some intersection of that row cluster. `tile_target`: every target block of a column cluster has a used entry in some intersection of that column cluster. `tile_count`: in every draw some intersection uses all 256 entries.
All inputs are finite; a program needn't handle non-finite values.
Results may differ from the reference program's by a relative error of at most 0.0003.
Values sent between devices are 32-bit elements; how exact they have to be, the bound alone decides.
No kernel may reach another device: no remote copies, remote signals or barrier semaphores. Data moves between devices by JAX's collectives and lax.ppermute only.
A program may use at most 256 MiB of HBM per device.

```python
import jax
import jax.numpy as jnp
from jax import lax

PC = 32
BLK = 256
SB_DEV = 256
TB_DEV = 8
CAP = 256
ROW_CELLS = 65536
COL_CELLS = 2048
SOURCE_CELLS = 524288
TARGET_CELLS = 65536
N_ROW = 8
N_COL = 32


def support_lists(key):
    counts = jax.random.randint(jax.random.fold_in(key, 101), (N_ROW, N_COL), CAP // 4, CAP // 2 + 1)
    busiest = jax.random.randint(jax.random.fold_in(key, 102), (), 0, N_ROW * N_COL)
    device_number = jnp.arange(N_ROW * N_COL, dtype=jnp.int32).reshape(N_ROW, N_COL)
    counts = jnp.where(device_number == busiest, CAP, counts).astype(jnp.int32)
    per_column = SB_DEV // N_COL
    home_count = max(per_column, TB_DEV)
    pair_total = SB_DEV * TB_DEV
    slot_index = jnp.arange(CAP, dtype=jnp.int32)
    pair_range = jnp.arange(pair_total, dtype=jnp.int32)

    def one_device(device, live_count):
        column = device % N_COL
        own_key = jax.random.fold_in(jax.random.fold_in(key, 103), device)
        home_steps = jnp.arange(home_count, dtype=jnp.int32)
        home_ids = (column + N_COL * (home_steps % per_column)) * TB_DEV + home_steps % TB_DEV
        shuffled = jax.random.permutation(jax.random.fold_in(own_key, 1), pair_total).astype(jnp.int32)
        block_source = shuffled // TB_DEV
        block_target = shuffled % TB_DEV
        cycle = block_source // N_COL
        if per_column >= TB_DEV:
            is_home = (block_source % N_COL == column) & (cycle % TB_DEV == block_target)
        else:
            is_home = (block_source % N_COL == column) & (block_target % per_column == cycle)
        order_key = jnp.where(is_home, pair_total + pair_range, pair_range)
        others = shuffled[jnp.argsort(order_key)][:CAP - home_count]
        listed = jnp.concatenate([home_ids, others])
        ranking = jax.random.permutation(jax.random.fold_in(own_key, 2), CAP).astype(jnp.int32)
        placing = jnp.where(slot_index < live_count, ranking, CAP + slot_index)
        return listed[jnp.argsort(placing)]
    tile_lists = jax.vmap(one_device)(jnp.arange(N_ROW * N_COL, dtype=jnp.int32), counts.reshape(-1))
    return (tile_lists.reshape(N_ROW, N_COL, CAP), counts)


def draw_tile_source(key, part):
    tile_lists, counts = support_lists(key)
    return (tile_lists // TB_DEV).astype(jnp.int32)


def draw_tile_target(key, part):
    tile_lists, counts = support_lists(key)
    return (tile_lists % TB_DEV).astype(jnp.int32)


def draw_tile_count(key, part):
    tile_lists, counts = support_lists(key)
    return counts


def draw_source_mass(key, part):
    key = jax.random.fold_in(key, 7)
    shape = (N_ROW * SB_DEV * BLK,)
    values = jax.random.uniform(jax.random.fold_in(key, 1), shape, jnp.float32, -12.0, -8.0)
    return values


def draw_target_potential(key, part):
    key = jax.random.fold_in(key, 9)
    shape = (N_COL * TB_DEV * BLK,)
    values = jnp.clip(jax.random.normal(jax.random.fold_in(key, 1), shape, jnp.float32), -4.0, 4.0)
    return values


def block_scale(rng, dims, pieces, low, largest):
    def one(position, blocks):
        heights = jax.random.uniform(jax.random.fold_in(jax.random.fold_in(rng, 6), position), (blocks,), jnp.float32, low / len(pieces), largest / len(pieces))
        return jnp.repeat(jnp.exp(heights), dims[position] // blocks).reshape((-1,) + (1,) * (len(dims) - position - 1))

    factor_of = one(*pieces[0])
    for cut in pieces[1:]:
        factor_of = factor_of * one(*cut)
    return factor_of


def bell_draw(rng, extent, scale, bound, split=(), kind=jnp.bfloat16):
    result = scale * jax.random.normal(rng, extent, jnp.float32)
    if split:
        result = result * block_scale(rng, extent, split, -0.22, 0.18)
    return jnp.clip(result, -bound, bound).astype(kind)


def setup_inputs(seed: int = 0) -> dict:
    key_list = jax.random.split(jax.random.key(seed), 11)
    source_coords = bell_draw(key_list[0], (PC, SOURCE_CELLS), 1.0, 6.0, ((1, 8),))
    target_coords = bell_draw(key_list[1], (PC, TARGET_CELLS), 1.0, 6.0, ((1, 32),))
    source_order = jax.vmap(lambda own: jax.random.permutation(own, ROW_CELLS))(jax.random.split(key_list[2], N_ROW)).reshape((N_ROW, ROW_CELLS)).astype(jnp.int32)
    target_order = jax.vmap(lambda own: jax.random.permutation(own, COL_CELLS))(jax.random.split(key_list[3], N_COL)).reshape((N_COL, COL_CELLS)).astype(jnp.int32)
    source_mass = draw_source_mass(jax.random.fold_in(key_list[10], 71), 0)
    target_mass = jnp.clip(-12.0 + 4.0 * jax.random.uniform(key_list[5], (TARGET_CELLS,), jnp.float32) ** block_scale(key_list[5], (TARGET_CELLS,), ((0, 32),), -0.2, 0.2), -12.0, -8.0)
    target_potential = draw_target_potential(jax.random.fold_in(key_list[10], 71), 0)
    tile_source = draw_tile_source(jax.random.fold_in(key_list[10], 71), 0)
    tile_target = draw_tile_target(jax.random.fold_in(key_list[10], 71), 0)
    tile_count = draw_tile_count(jax.random.fold_in(key_list[10], 71), 0)
    return {"source_coords": source_coords, "target_coords": target_coords, "source_order": source_order, "target_order": target_order, "source_mass": source_mass, "target_mass": target_mass, "target_potential": target_potential, "tile_source": tile_source, "tile_target": tile_target, "tile_count": tile_count}


epsilon = 0.1
very_negative = -1.0e30
tile_group = 8


def blocked_index(order, cells_each):
    offsets = jnp.arange(order.shape[0], dtype=jnp.int32)[:, None] * cells_each
    return (order.astype(jnp.int32) + offsets).reshape(-1)


def tile_costs(source_blocks, source_norm, target_blocks, target_norm, which_source, which_target):
    left_block = jnp.take(source_blocks, which_source, axis=1).astype(jnp.float32)
    right_block = jnp.take(target_blocks, which_target, axis=1).astype(jnp.float32)
    products = jnp.einsum("dgi,dgj->gij", left_block, right_block, precision=lax.Precision.HIGHEST)
    return (source_norm[which_source][:, :, None] + target_norm[which_target][None, :, :][0][:, None, :] - 2.0 * products) / PC


def reference(source_coords, target_coords, source_order, target_order, source_mass, target_mass, target_potential, tile_source, tile_target, tile_count):
    source_index = blocked_index(source_order, SB_DEV * BLK)
    target_index = blocked_index(target_order, TB_DEV * BLK)
    source_blocks = jnp.take(source_coords, source_index, axis=1).reshape(PC, N_ROW * SB_DEV, BLK)
    target_blocks = jnp.take(target_coords, target_index, axis=1).reshape(PC, N_COL * TB_DEV, BLK)
    source_norm = jnp.sum(jnp.square(source_blocks.astype(jnp.float32)), axis=0)
    target_norm = jnp.sum(jnp.square(target_blocks.astype(jnp.float32)), axis=0)
    source_weight = source_mass[source_index].reshape(N_ROW * SB_DEV, BLK)
    target_weight = target_mass[target_index].reshape(N_COL * TB_DEV, BLK)
    start_potential = target_potential[target_index].reshape(N_COL * TB_DEV, BLK)
    row_offset = jnp.arange(N_ROW, dtype=jnp.int32)[:, None, None] * SB_DEV
    col_offset = jnp.arange(N_COL, dtype=jnp.int32)[None, :, None] * TB_DEV
    global_source = (tile_source.astype(jnp.int32) + row_offset).reshape(-1)
    global_target = (tile_target.astype(jnp.int32) + col_offset).reshape(-1)
    active = (jnp.arange(CAP, dtype=jnp.int32)[None, None, :] < tile_count[:, :, None]).reshape(-1)
    groups = global_source.shape[0] // tile_group
    grouped = (global_source.reshape(groups, tile_group), global_target.reshape(groups, tile_group), active.reshape(groups, tile_group))

    def row_step(group_data):
        which_source, which_target, active_group = group_data
        tile_cost = tile_costs(source_blocks, source_norm, target_blocks, target_norm, which_source, which_target)
        scores = (start_potential[which_target][:, None, :] - tile_cost) / epsilon
        highest = jnp.max(scores, axis=2)
        summed = jnp.sum(jnp.exp(scores - highest[:, :, None]), axis=2)
        return (jnp.where(active_group[:, None], highest, very_negative), jnp.where(active_group[:, None], summed, 0.0))

    tile_max, tile_sum = lax.map(row_step, grouped)
    tile_max = tile_max.reshape(-1, BLK)
    tile_sum = tile_sum.reshape(-1, BLK)
    row_max = jnp.full((N_ROW * SB_DEV, BLK), very_negative, jnp.float32).at[global_source].max(tile_max)
    row_sum = jnp.zeros((N_ROW * SB_DEV, BLK), jnp.float32).at[global_source].add(tile_sum * jnp.exp(tile_max - row_max[global_source]))
    source_dual = epsilon * source_weight - epsilon * (row_max + jnp.log(row_sum))

    def col_step(group_data):
        which_source, which_target, active_group = group_data
        tile_cost = tile_costs(source_blocks, source_norm, target_blocks, target_norm, which_source, which_target)
        scores = (source_dual[which_source][:, :, None] - tile_cost) / epsilon
        highest = jnp.max(scores, axis=1)
        summed = jnp.sum(jnp.exp(scores - highest[:, None, :]), axis=1)
        return (jnp.where(active_group[:, None], highest, very_negative), jnp.where(active_group[:, None], summed, 0.0))

    col_tile_max, col_tile_sum = lax.map(col_step, grouped)
    col_tile_max = col_tile_max.reshape(-1, BLK)
    col_tile_sum = col_tile_sum.reshape(-1, BLK)
    col_max = jnp.full((N_COL * TB_DEV, BLK), very_negative, jnp.float32).at[global_target].max(col_tile_max)
    col_sum = jnp.zeros((N_COL * TB_DEV, BLK), jnp.float32).at[global_target].add(col_tile_sum * jnp.exp(col_tile_max - col_max[global_target]))
    target_dual = epsilon * target_weight - epsilon * (col_max + jnp.log(col_sum))
    source_update = jnp.zeros((source_index.shape[0],), jnp.float32).at[source_index].set(source_dual.reshape(-1))
    target_update = jnp.zeros((target_index.shape[0],), jnp.float32).at[target_index].set(target_dual.reshape(-1))
    return (source_update, target_update)
```

```python
import functools
import math

import jax
import jax.numpy as jnp
from jax import lax
from jax.experimental import pallas as pl
from jax.experimental.pallas import tpu as pltpu
from jax.sharding import PartitionSpec as P

PC = 32
BLK = 256
Z = 8
Y = 4
ROWS = 8
SRC = 65536
TGT = 2048
CHUNK = SRC // Y
NB = CHUNK // BLK
TB = TGT // BLK
CAP = 256
PACK = 40
LOG2E = math.log2(math.e)
KAPPA = 10.0 * LOG2E
LN2 = math.log(2.0)
LOW = -1e30

f32 = jnp.float32
bf16 = jnp.bfloat16
NT = (((1,), (1,)), ((), ()))


def iota(shape, axis):
    return lax.broadcasted_iota(jnp.int32, shape, axis)


def indicator(condition):
    return jnp.where(condition, 1.0, 0.0).astype(bf16)


def three(value):
    first = value.astype(bf16).astype(f32)
    rest = value - first
    second = rest.astype(bf16).astype(f32)
    return first, second, rest - second


def vmem():
    return pl.BlockSpec(memory_space=pltpu.VMEM)


def smem():
    return pl.BlockSpec(memory_space=pltpu.SMEM)


def call(kernel, name, out_shape, in_specs, scratch, flops=0, nbytes=0, exps=0, limit=48):
    many = isinstance(out_shape, (list, tuple))
    return pl.pallas_call(
        kernel,
        out_shape=out_shape,
        in_specs=in_specs,
        out_specs=[vmem() for _ in out_shape] if many else vmem(),
        scratch_shapes=scratch,
        compiler_params=pltpu.CompilerParams(vmem_limit_bytes=limit * 2**20),
        cost_estimate=pl.CostEstimate(flops=flops, bytes_accessed=nbytes, transcendentals=exps),
        name=name,
    )


def target_kernel(coords, order, potential, which_source, which_target, count, out, left):
    sub8 = iota((8, TGT), 0)
    vh, vm, vl = three(jnp.broadcast_to(potential[...], (8, TGT)))
    part = jnp.where(sub8 == 0, vh, jnp.where(sub8 == 1, vm, jnp.where(sub8 == 2, vl, 0.0)))
    left[0:32, :] = coords[...]
    left[32:48, :] = jnp.concatenate([part, jnp.zeros((8, TGT), f32)], axis=0).astype(bf16)
    number = iota((TGT, BLK), 0)

    def one_block(b, carry):
        span = pl.ds(pl.multiple_of(b * BLK, BLK), BLK)
        picked = indicator(number == order[:, span])
        got = jnp.dot(left[...], picked, preferred_element_type=f32)
        y = got[0:32]
        v = got[32:33] + got[33:34] + got[34:35]
        a = (v - jnp.sum(y * y, axis=0, keepdims=True) * (1.0 / PC)) * KAPPA
        out[0:32, span] = y
        out[32:40, span] = jnp.broadcast_to(a, (8, BLK))
        return carry

    lax.fori_loop(0, TB, one_block, 0)

    src = which_source[...]
    used = iota((1, CAP), 1) < count[0, 0]
    quarter = jnp.where(used, src // NB, 7)
    member = jnp.where(iota((8, CAP), 0) == quarter, 1.0, 0.0)
    earlier = indicator(iota((CAP, CAP), 0) < iota((CAP, CAP), 1))
    before = jnp.dot(member.astype(bf16), earlier, preferred_element_type=f32)
    rank = jnp.sum(member * before, axis=0, keepdims=True).astype(jnp.int32)
    place = quarter * CAP + rank
    sub16 = iota((16, CAP), 0)
    code = jnp.where(
        sub16 == 0,
        ((src % NB) * 8).astype(f32),
        jnp.where(sub16 == 1, (which_target[...] + 1).astype(f32), 0.0),
    ).astype(bf16)
    chosen = indicator(iota((Y * CAP, CAP), 0) == place)
    listed = lax.dot_general(code, chosen, NT, preferred_element_type=f32)
    out[39:40, 0 : Y * CAP] = listed[0:1] + listed[1:2]
    out[39:40, Y * CAP :] = jnp.zeros((1, TGT - Y * CAP), f32)


def gather_kernel(coords, mass, order, out, table, rows):
    sub8 = iota((8, 128), 0)
    lane = lax.rem(sub8, 4)
    tail = jnp.concatenate([jnp.where(sub8 == 0, 1.0, 0.0), jnp.zeros((16, 128), f32)], axis=0)

    def build(b):
        span = pl.ds(pl.multiple_of(b * 128, 128), 128)
        x = coords[:, span].astype(f32)
        norm = jnp.sum(x * x, axis=0, keepdims=True) * (-KAPPA / PC)
        weight = mass[pl.ds(b, 1), :] * LOG2E
        both = jnp.where(sub8 < 4, jnp.broadcast_to(norm, (8, 128)), jnp.broadcast_to(weight, (8, 128)))
        h, m, l = three(both)
        part = jnp.where(lane == 0, h, jnp.where(lane == 1, m, jnp.where(lane == 2, l, 1.0)))
        table[span, :] = jnp.concatenate([x, x, x, part, tail], axis=0).T

    def build_four(g, carry):
        for u in range(4):
            build(g * 4 + u)
        return carry

    lax.fori_loop(0, SRC // 512, build_four, 0)

    def one_block(b, carry):
        base = b * BLK
        for i in range(BLK):
            rows[pl.ds(i, 1), :] = table[pl.ds(order[0, base + i], 1), :]
        out[pl.ds(pl.multiple_of(base, BLK), BLK), :] = rows[...].astype(bf16)
        return carry

    lax.fori_loop(0, NB, one_block, 0)


def tiles(left_of, right_of, slot_of, highest, total, counts, codes):
    def tile(d, e):
        code = codes[d, e]
        s, t = code // 8, lax.rem(code, 8)
        score = lax.dot_general(left_of(d, s, t), right_of(d, s, t), NT, preferred_element_type=f32)
        top = jnp.max(score, axis=0, keepdims=True)
        return slot_of(d, s, t), top, jnp.sum(jnp.exp2(score - top), axis=0, keepdims=True)

    def add(slot, top, summed):
        for half in range(2):
            here, there = pl.ds(2 * slot + half, 1), slice(half * 128, half * 128 + 128)
            old = highest[here, :]
            new = jnp.maximum(old, top[:, there])
            total[here, :] = total[here, :] * jnp.exp2(old - new) + summed[:, there] * jnp.exp2(top[:, there] - new)
            highest[here, :] = new

    highest[...] = jnp.full(highest.shape, LOW, f32)
    total[...] = jnp.zeros(total.shape, f32)
    for d in range(Y):
        count = counts[d]

        def pair(g, carry):
            first = tile(d, 2 * g)
            has = 2 * g + 1 < count
            slot, top, summed = tile(d, jnp.where(has, 2 * g + 1, 2 * g))
            add(*first)
            add(slot, jnp.where(has, top, LOW), jnp.where(has, summed, 0.0))
            return carry

        lax.fori_loop(0, (count + 1) // 2, pair, 0)
    return jnp.where(total[...] > 0.0, highest[...] + jnp.log2(total[...]), LOW)


def row_kernel(source, p0, p1, p2, p3, codes, counts, partial, late, early, highest, total):
    lane = iota((128, 128), 1)
    turned = ((lane >= 100) & (lane <= 102)) | ((lane >= 105) & (lane <= 107))
    sub8 = iota((8, 128), 0)
    for d, pack in enumerate((p0, p1, p2, p3)):

        def build(b, carry):
            span = pl.ds(pl.multiple_of(b * 128, 128), 128)
            h, m, l = three(pack[0:32, span] * (KAPPA / 16.0))
            ah, am, al = three(jnp.broadcast_to(pack[32:33, span], (8, 128)))
            part = jnp.where(sub8 < 3, 1.0, jnp.where(sub8 == 3, ah, jnp.where(sub8 == 7, am, 0.0)))
            last = jnp.where(sub8 == 0, al, 0.0)
            rows = jnp.concatenate([h, m, l, part, last, jnp.zeros((16, 128), f32)], axis=0).T
            place = pl.ds(pl.multiple_of(d * TGT + b * 128, 128), 128)
            early[place, :] = rows.astype(bf16)
            late[place, :] = jnp.where(turned, 1.0, rows).astype(bf16)
            return carry

        lax.fori_loop(0, TGT // 128, build, 0)

    partial[...] = tiles(
        lambda d, s, t: early[pl.ds(pl.multiple_of(d * TGT + t * BLK, BLK), BLK), :],
        lambda d, s, t: source[pl.ds(pl.multiple_of(s * BLK, BLK), BLK), :],
        lambda d, s, t: s,
        highest,
        total,
        counts,
        codes,
    )


def merged(parts):
    top = functools.reduce(jnp.maximum, parts)
    return top + jnp.log2(sum(jnp.exp2(part - top) for part in parts))


def merge_kernel(*refs):
    refs[-1][...] = merged([ref[...] for ref in refs[:-1]])


def col_kernel(source, late, lse, codes, counts, partial, filled, highest, total):
    sub8 = iota((8, 128), 0)

    def fill(b, carry):
        for half in range(2):
            row = -lse[pl.ds(2 * b + half, 1), :]
            h, m, l = three(jnp.broadcast_to(row, (8, 128)))
            part = jnp.where(sub8 == 1, h, jnp.where(sub8 == 2, m, jnp.where(sub8 == 3, l, 0.0)))
            rows = jnp.concatenate([jnp.zeros((104, 128), f32), part, jnp.zeros((16, 128), f32)], axis=0).T
            span = pl.ds(pl.multiple_of(b * BLK + half * 128, 128), 128)
            filled[span, :] = source[span, :] + rows.astype(bf16)
        return carry

    lax.fori_loop(0, NB, fill, 0)
    partial[...] = tiles(
        lambda d, s, t: filled[pl.ds(pl.multiple_of(s * BLK, BLK), BLK), :],
        lambda d, s, t: late[pl.ds(pl.multiple_of(d * TGT + t * BLK, BLK), BLK), :],
        lambda d, s, t: d * TB + t,
        highest,
        total,
        counts,
        codes,
    )


def flat(block):
    return jnp.concatenate([block[u : u + 1, :] for u in range(8)], axis=1)


def spread(order_row, value_row, high_rows):
    n = order_row.shape[1]
    high = indicator(iota((high_rows, n), 0) == order_row // 128)
    match = iota((128, n), 0) == lax.rem(order_row, 128)
    first = value_row.astype(bf16).astype(f32)
    low = jnp.concatenate(
        [jnp.where(match, first, 0.0), jnp.where(match, value_row - first, 0.0)], axis=0
    ).astype(bf16)
    return lax.dot_general(high, low, NT, preferred_element_type=f32)


def source_kernel(order, l0, l1, l2, l3, chunks, mass, out, total):
    total[...] = jnp.zeros(total.shape, f32)
    for d, lse in enumerate((l0, l1, l2, l3)):
        first = chunks[d] * (2 * NB)

        def step(g, carry):
            where = order[pl.ds(pl.multiple_of(first + g * 8, 8), 8), :]
            value = lse[pl.ds(pl.multiple_of(g * 8, 8), 8), :]
            total[...] += spread(flat(where), flat(value), SRC // 128)
            return carry

        lax.fori_loop(0, NB // 4, step, 0)
    out[...] = 0.1 * mass[...] - (0.1 * LN2) * (total[:, 0:128] + total[:, 128:256])


def final_kernel(*refs):
    order, mass, potential, out = refs[8:12]
    lse = merged([ref[...] for ref in refs[:8]])
    total = jnp.zeros((TGT // 128, 256), f32)
    for g in range(TGT // 1024):
        total += spread(flat(order[g * 8 : g * 8 + 8, :]), flat(lse[g * 8 : g * 8 + 8, :]), TGT // 128)
    out[...] = 0.1 * mass[...] + potential[...] - (0.1 * LN2) * (total[:, 0:128] + total[:, 128:256])


def y_shift(d):
    return [(z * Y + y, z * Y + (y + d) % Y) for z in range(Z) for y in range(Y)]


def z_shift(d):
    return [(z * Y + y, (z + d) % Z * Y + y) for z in range(Z) for y in range(Y)]


def row_shift(d):
    return [(r, (r + d) % ROWS) for r in range(ROWS)]


def body(
    source_coords,
    target_coords,
    source_order,
    target_order,
    source_mass,
    target_mass,
    target_potential,
    tile_source,
    tile_target,
    tile_count,
):
    shape = jax.ShapeDtypeStruct
    y = lax.rem(lax.axis_index("col"), Y)
    mass = source_mass.reshape(SRC // 128, 128)

    pack = call(
        target_kernel,
        "target_gather",
        shape((PACK, TGT), f32),
        [vmem()] * 5 + [smem()],
        [pltpu.VMEM((48, TGT), bf16)],
        flops=2 * 48 * TGT * TGT,
    )(
        target_coords,
        target_order,
        target_potential.reshape(1, TGT),
        tile_source.reshape(1, CAP),
        tile_target.reshape(1, CAP),
        tile_count,
    )
    packs = [pack] + [lax.ppermute(pack, "col", y_shift(d)) for d in range(1, Y)]

    source = call(
        gather_kernel,
        "source_gather",
        shape((CHUNK, 128), bf16),
        [vmem(), vmem(), smem()],
        [pltpu.VMEM((SRC, 128), f32), pltpu.VMEM((BLK, 128), f32)],
        flops=2 * 10**10,
        nbytes=64 * 2**20,
        limit=56,
    )(source_coords, mass, lax.dynamic_slice(source_order, (0, y * CHUNK), (1, CHUNK)))

    lists = jnp.concatenate([lax.dynamic_slice(p, (PACK - 1, y * CAP), (1, CAP)) for p in packs], axis=0)
    codes = lists.astype(jnp.int32) - 1
    counts = jnp.sum((lists > 0.5).astype(jnp.int32), axis=1)

    partial, late = call(
        row_kernel,
        "row_pass",
        [shape((2 * NB, 128), f32), shape((Y * TGT, 128), bf16)],
        [vmem()] * 5 + [smem()] * 2,
        [pltpu.VMEM((Y * TGT, 128), bf16), pltpu.VMEM((2 * NB, 128), f32), pltpu.VMEM((2 * NB, 128), f32)],
    )(source, *packs, codes, counts)

    partials = [partial] + [lax.ppermute(partial, "col", z_shift(d)) for d in range(1, Z)]
    lse = call(merge_kernel, "row_merge", shape((2 * NB, 128), f32), [vmem()] * Z, [])(*partials)
    lses = [lse] + [lax.ppermute(lse, "col", y_shift(d)) for d in range(1, Y)]

    target_partial = call(
        col_kernel,
        "col_pass",
        shape((2 * Y * TB, 128), f32),
        [vmem()] * 3 + [smem()] * 2,
        [
            pltpu.VMEM((CHUNK, 128), bf16),
            pltpu.VMEM((2 * Y * TB, 128), f32),
            pltpu.VMEM((2 * Y * TB, 128), f32),
        ],
        flops=2 * 10**10,
        exps=10**7,
    )(source, late, lse, codes, counts)

    own = [target_partial[0 : 2 * TB]] + [
        lax.ppermute(target_partial[2 * d * TB : 2 * (d + 1) * TB], "col", y_shift(-d)) for d in range(1, Y)
    ]
    own = call(merge_kernel, "col_merge", shape((2 * TB, 128), f32), [vmem()] * Y, [])(*own)
    all_rows = [own] + [lax.ppermute(own, "row", row_shift(d)) for d in range(1, ROWS)]

    chunks = lax.rem(y + Y - jnp.arange(Y, dtype=jnp.int32), Y)
    source_update = call(
        source_kernel,
        "source_scatter",
        shape((SRC // 128, 128), f32),
        [vmem()] * 5 + [smem(), vmem()],
        [pltpu.VMEM((SRC // 128, 256), f32)],
        flops=2 * 512 * 256 * SRC,
        nbytes=2**20,
    )(source_order.reshape(SRC // 128, 128), *lses, chunks, mass)

    target_update = call(
        final_kernel,
        "target_scatter",
        shape((TGT // 128, 128), f32),
        [vmem()] * 11,
        [],
    )(
        *all_rows,
        target_order.reshape(TGT // 128, 128),
        target_mass.reshape(TGT // 128, 128),
        target_potential.reshape(TGT // 128, 128),
    )
    return (source_update.reshape(SRC), target_update.reshape(TGT))


def solution(mesh):
    in_specs = (
        P(None, "row"),
        P(None, "col"),
        P("row", None),
        P("col", None),
        P("row"),
        P("col"),
        P("col"),
        P("row", "col", None),
        P("row", "col", None),
        P("row", "col"),
    )
    out_specs = (P("row"), P("col"))
    return jax.shard_map(body, mesh=mesh, in_specs=in_specs, out_specs=out_specs, check_vma=False)
```

```python
import functools
import math

import jax
import jax.numpy as jnp
from jax import lax
from jax.experimental import pallas as pl
from jax.experimental.pallas import tpu as pltpu
from jax.sharding import PartitionSpec as P

PC = 32
BLK = 256
Z = 8
Y = 4
ROWS = 8
SRC = 65536
TGT = 2048
CHUNK = SRC // Y
NB = CHUNK // BLK
TB = TGT // BLK
CAP = 256
UNROLL = 8
SCATTER = 8
BUILD = 32
LOADS = 4
STORES = 4
PACK = 40
LOG2E = math.log2(math.e)
KAPPA = 10.0 * LOG2E
LN2 = math.log(2.0)
LOW = -1e30

f32 = jnp.float32
bf16 = jnp.bfloat16
NT = (((1,), (1,)), ((), ()))


def iota(shape, axis):
    return lax.broadcasted_iota(jnp.int32, shape, axis)


def indicator(condition):
    return jnp.where(condition, 1.0, 0.0).astype(bf16)


def three(value):
    first = value.astype(bf16).astype(f32)
    rest = value - first
    second = rest.astype(bf16).astype(f32)
    return first, second, rest - second


def vmem():
    return pl.BlockSpec(memory_space=pltpu.VMEM)


def anywhere():
    return pl.BlockSpec(memory_space=pl.ANY)


def smem():
    return pl.BlockSpec(memory_space=pltpu.SMEM)


def call(kernel, name, out_shape, in_specs, scratch, flops=0, nbytes=0, exps=0, limit=48, out_specs=None):
    many = isinstance(out_shape, (list, tuple))
    return pl.pallas_call(
        kernel,
        out_shape=out_shape,
        in_specs=in_specs,
        out_specs=out_specs or ([vmem() for _ in out_shape] if many else vmem()),
        scratch_shapes=scratch,
        compiler_params=pltpu.CompilerParams(vmem_limit_bytes=limit * 2**20),
        cost_estimate=pl.CostEstimate(flops=flops, bytes_accessed=nbytes, transcendentals=exps),
        name=name,
    )


def target_kernel(*refs):
    given, count, out, left, held, sems = refs[:5], refs[5], refs[6], refs[7], refs[8:13], refs[13]
    loads = [pltpu.make_async_copy(here, there, sems.at[k]) for k, (here, there) in enumerate(zip(given, held))]
    for load in loads:
        load.start()
    for load in loads:
        load.wait()
    coords, order, potential, which_source, which_target = held
    sub8 = iota((8, TGT), 0)
    vh, vm, vl = three(jnp.broadcast_to(potential[...], (8, TGT)))
    part = jnp.where(sub8 == 0, vh, jnp.where(sub8 == 1, vm, jnp.where(sub8 == 2, vl, 0.0)))
    left[0:32, :] = coords[...]
    left[32:48, :] = jnp.concatenate([part, jnp.zeros((8, TGT), f32)], axis=0).astype(bf16)
    number = iota((TGT, BLK), 0)

    def one_block(b, carry):
        span = pl.ds(pl.multiple_of(b * BLK, BLK), BLK)
        picked = indicator(number == order[:, span])
        got = jnp.dot(left[...], picked, preferred_element_type=f32)
        y = got[0:32]
        v = got[32:33] + got[33:34] + got[34:35]
        a = (v - jnp.sum(y * y, axis=0, keepdims=True) * (1.0 / PC)) * KAPPA
        out[0:32, span] = y
        out[32:40, span] = jnp.broadcast_to(a, (8, BLK))
        return carry

    lax.fori_loop(0, TB, one_block, 0)

    src = which_source[...]
    used = iota((1, CAP), 1) < count[0, 0]
    quarter = jnp.where(used, src // NB, 7)
    member = jnp.where(iota((8, CAP), 0) == quarter, 1.0, 0.0)
    earlier = indicator(iota((CAP, CAP), 0) < iota((CAP, CAP), 1))
    before = jnp.dot(member.astype(bf16), earlier, preferred_element_type=f32)
    rank = jnp.sum(member * before, axis=0, keepdims=True).astype(jnp.int32)
    place = quarter * CAP + rank
    sub16 = iota((16, CAP), 0)
    code = jnp.where(
        sub16 == 0,
        ((src % NB) * 8).astype(f32),
        jnp.where(sub16 == 1, (which_target[...] + 1).astype(f32), 0.0),
    ).astype(bf16)
    chosen = indicator(iota((Y * CAP, CAP), 0) == place)
    listed = lax.dot_general(code, chosen, NT, preferred_element_type=f32)
    out[39:40, 0 : Y * CAP] = listed[0:1] + listed[1:2]
    out[39:40, Y * CAP :] = jnp.zeros((1, TGT - Y * CAP), f32)


def gather_kernel(coords_all, mass_all, order_all, out_all, table, rows, coords, mass, order, out, sems, in_sem, out_sem):
    start = pl.multiple_of(lax.rem(lax.axis_index("col"), Y) * CHUNK, CHUNK)
    share = SRC // LOADS
    weights = pltpu.make_async_copy(mass_all, mass, in_sem.at[0])
    listed = pltpu.make_async_copy(order_all.at[:, pl.ds(start, CHUNK)], order, in_sem.at[1])
    loads = [
        pltpu.make_async_copy(
            coords_all.at[:, k * share : (k + 1) * share], coords.at[:, k * share : (k + 1) * share], sems.at[k]
        )
        for k in range(LOADS)
    ]
    weights.start()
    for load in loads:
        load.start()
    listed.start()
    sub8 = iota((8, 128), 0)
    lane = lax.rem(sub8, 4)
    first = jnp.where(sub8 == 0, 1.0, 0.0)
    blank = jnp.zeros((16, 128), bf16)

    def build(b):
        span = pl.ds(pl.multiple_of(b * 128, 128), 128)
        x = coords[:, span]
        wide = x.astype(f32)
        norm = jnp.sum(wide * wide, axis=0, keepdims=True) * (-KAPPA / PC)
        weight = mass[pl.ds(b, 1), :] * LOG2E
        both = jnp.where(sub8 < 4, jnp.broadcast_to(norm, (8, 128)), jnp.broadcast_to(weight, (8, 128)))
        h, m, l = three(both)
        part = jnp.where(lane == 0, h, jnp.where(lane == 1, m, jnp.where(lane == 2, l, 1.0)))
        part = jnp.concatenate([part, first], axis=0).astype(bf16)
        table[span, :] = jnp.concatenate([x, x, x, part, blank], axis=0).T.astype(f32)

    weights.wait()
    for k in range(LOADS):
        loads[k].wait()

        def several(g, carry):
            for u in range(BUILD):
                build(k * (share // 128) + g * BUILD + u)
            return carry

        lax.fori_loop(0, share // 128 // BUILD, several, 0)

    listed.wait()

    def one_block(b, carry):
        base = b * BLK
        for i in range(BLK):
            rows[pl.ds(i, 1), :] = table[pl.ds(order[0, base + i], 1), :]
        out[pl.ds(pl.multiple_of(base, BLK), BLK), :] = rows[...].astype(bf16)
        return carry

    share = CHUNK // STORES
    stores = []
    for k in range(STORES):
        lax.fori_loop(k * (NB // STORES), (k + 1) * (NB // STORES), one_block, 0)
        here = slice(k * share, (k + 1) * share)
        stores.append(pltpu.make_async_copy(out.at[here, :], out_all.at[here, :], out_sem.at[k]))
        stores[-1].start()
    for store in stores:
        store.wait()


def tiles(left_of, right_of, slot_of, highest, total, counts, codes, entries):
    filled = 0
    for d in range(Y):

        def copy(e, base):
            code = codes[d, e]
            entries[base + e] = code + (code // 8) * (TB * (Y - 1)) + d * TB
            return base

        lax.fori_loop(0, counts[d], copy, filled)
        filled = filled + counts[d]

    def tile(e):
        code = entries[e]
        s, t = code // (Y * TB), lax.rem(code, Y * TB)
        left = left_of(s, t)
        found = []
        for half in range(2):
            score = lax.dot_general(left, right_of(s, t, half), NT, preferred_element_type=f32)
            top = jnp.max(score, axis=0, keepdims=True)
            found.append((top, jnp.sum(jnp.exp2(score - top), axis=0, keepdims=True)))
        return slot_of(s, t), found

    def add(slot, found, has):
        for half, (top, summed) in enumerate(found):
            here = pl.ds(2 * slot + half, 1)
            top = jnp.where(has, top, LOW)
            old = highest[here, :]
            new = jnp.maximum(old, top)
            summed = jnp.where(has, summed, 0.0)
            total[here, :] = total[here, :] * jnp.exp2(old - new) + summed * jnp.exp2(top - new)
            highest[here, :] = new

    highest[...] = jnp.full(highest.shape, LOW, f32)
    total[...] = jnp.zeros(total.shape, f32)

    def several(g, carry):
        found = [tile(jnp.minimum(g * UNROLL + u, filled - 1)) for u in range(UNROLL)]
        for u in range(UNROLL):
            add(*found[u], g * UNROLL + u < filled)
        return carry

    lax.fori_loop(0, (filled + UNROLL - 1) // UNROLL, several, 0)
    return jnp.where(total[...] > 0.0, highest[...] + jnp.log2(total[...]), LOW)


def row_kernel(
    source_all, p0, p1, p2, p3, codes, counts, partial, late_all, source, late, early, highest, total, entries, sem
):
    load = pltpu.make_async_copy(source_all, source, sem.at[0])
    load.start()
    lane = iota((128, 128), 1)
    turned = indicator(((lane >= 100) & (lane <= 102)) | ((lane >= 105) & (lane <= 107)))
    sub8 = iota((8, 128), 0)
    for d, pack in enumerate((p0, p1, p2, p3)):

        def build(b, carry):
            span = pl.ds(pl.multiple_of(b * 128, 128), 128)
            h, m, l = three(pack[0:32, span] * (KAPPA / 16.0))
            ah, am, al = three(jnp.broadcast_to(pack[32:33, span], (8, 128)))
            part = jnp.where(sub8 < 3, 1.0, jnp.where(sub8 == 3, ah, jnp.where(sub8 == 7, am, 0.0)))
            last = jnp.where(sub8 == 0, al, 0.0)
            rows = jnp.concatenate([h, m, l, part, last, jnp.zeros((16, 128), f32)], axis=0).astype(bf16).T
            place = pl.ds(pl.multiple_of(d * TGT + b * 128, 128), 128)
            early[place, :] = rows
            late[place, :] = rows + turned
            return carry

        lax.fori_loop(0, TGT // 128, build, 0)

    store = pltpu.make_async_copy(late, late_all, sem.at[1])
    store.start()
    load.wait()
    partial[...] = tiles(
        lambda s, t: early[pl.ds(pl.multiple_of(t * BLK, BLK), BLK), :],
        lambda s, t, half: source[pl.ds(pl.multiple_of(s * BLK + half * 128, 128), 128), :],
        lambda s, t: s,
        highest,
        total,
        counts,
        codes,
        entries,
    )
    store.wait()


def merged(parts):
    top = functools.reduce(jnp.maximum, parts)
    return top + jnp.log2(sum(jnp.exp2(part - top) for part in parts))


def merge_kernel(*refs):
    refs[-1][...] = merged([ref[...] for ref in refs[:-1]])


def col_kernel(source_all, late_all, lse, codes, counts, partial, filled, late, highest, total, entries, sems):
    share = CHUNK // LOADS
    second = pltpu.make_async_copy(late_all, late, sems.at[LOADS])
    loads = []
    for k in range(LOADS):
        here = slice(k * share, (k + 1) * share)
        loads.append(pltpu.make_async_copy(source_all.at[here, :], filled.at[here, :], sems.at[k]))
        loads[-1].start()
    second.start()
    sub8 = iota((8, 128), 0)

    def fill(g, carry):
        for u in range(4):
            row = -lse[pl.ds(g * 4 + u, 1), :]
            h, m, l = three(jnp.broadcast_to(row, (8, 128)))
            part = jnp.where(sub8 == 1, h, jnp.where(sub8 == 2, m, jnp.where(sub8 == 3, l, 0.0)))
            rows = jnp.concatenate([jnp.zeros((104, 128), f32), part, jnp.zeros((16, 128), f32)], axis=0)
            span = pl.ds(pl.multiple_of((g * 4 + u) * 128, 128), 128)
            filled[span, :] = filled[span, :] + rows.astype(bf16).T
        return carry

    for k in range(LOADS):
        loads[k].wait()
        lax.fori_loop(k * (share // 512), (k + 1) * (share // 512), fill, 0)
    second.wait()
    partial[...] = tiles(
        lambda s, t: filled[pl.ds(pl.multiple_of(s * BLK, BLK), BLK), :],
        lambda s, t, half: late[pl.ds(pl.multiple_of(t * BLK + half * 128, 128), 128), :],
        lambda s, t: t,
        highest,
        total,
        counts,
        codes,
        entries,
    )


def flat(block):
    return jnp.concatenate([block[u : u + 1, :] for u in range(8)], axis=1)


def spread(order_row, value_row, high_rows):
    n = order_row.shape[1]
    high = indicator(iota((high_rows, n), 0) == order_row // 128)
    match = iota((128, n), 0) == lax.rem(order_row, 128)
    first = value_row.astype(bf16).astype(f32)
    low = jnp.concatenate(
        [jnp.where(match, first, 0.0), jnp.where(match, value_row - first, 0.0)], axis=0
    ).astype(bf16)
    return lax.dot_general(high, low, NT, preferred_element_type=f32)


def scatter_kernel(is_first, mass, order, lse, chunk, *refs):
    out, total = refs[-2:]
    number = iota((256, 1024), 0).astype(f32).astype(bf16)
    one, zero = jnp.ones((), bf16), jnp.zeros((), bf16)
    first = chunk[0] * (2 * NB)
    if is_first:
        total[...] = jnp.zeros(total.shape, f32)
    else:
        total[...] = refs[0][...]

    def product(g):
        cell = flat(order[pl.ds(pl.multiple_of(first + g * 8, 8), 8), :])
        value = flat(lse[pl.ds(pl.multiple_of(g * 8, 8), 8), :])
        column = lax.rem(cell // 128, 256).astype(f32).astype(bf16)
        row = (cell // 32768 * 128 + lax.rem(cell, 128)).astype(f32).astype(bf16)
        big = value.astype(bf16)
        small = (value - big.astype(f32)).astype(bf16)
        match = number == row
        left = jnp.concatenate([jnp.where(match, big, zero), jnp.where(match, small, zero)], axis=0)
        right = jnp.where(number == column, one, zero)
        return lax.dot_general(left, right, NT, preferred_element_type=f32)

    def step(g, carry):
        total[...] += sum(product(g * SCATTER + u) for u in range(SCATTER))
        return carry

    lax.fori_loop(0, NB // 4 // SCATTER, step, 0)
    if mass is None:
        out[...] = total[...]
        return
    for half in range(2):
        for side in range(2):
            here, rows = slice(side * 128, side * 128 + 128), half * 128
            both = total[rows : rows + 128, here] + total[256 + rows : 384 + rows, here]
            here = slice(half * 256 + side * 128, half * 256 + side * 128 + 128)
            out[here, :] = 0.1 * mass[here, :] - (0.1 * LN2) * both.T


def last_scatter_kernel(mass, *refs):
    scatter_kernel(False, mass, *refs)


def final_kernel(*refs):
    order, mass, potential, out = refs[4:]
    lse = merged([ref[...] for ref in refs[:4]])
    total = jnp.zeros((TGT // 128, 256), f32)
    for g in range(TGT // 1024):
        total += spread(flat(order[g * 8 : g * 8 + 8, :]), flat(lse[g * 8 : g * 8 + 8, :]), TGT // 128)
    out[...] = 0.1 * mass[...] + potential[...] - (0.1 * LN2) * (total[:, 0:128] + total[:, 128:256])


def y_shift(d):
    return [(z * Y + y, z * Y + (y + d) % Y) for z in range(Z) for y in range(Y)]


def z_shift(d):
    return [(z * Y + y, (z + d) % Z * Y + y) for z in range(Z) for y in range(Y)]


def z_pair():
    return [(z * Y + y, (z ^ 1) * Y + y) for z in range(Z) for y in range(Y)]


def row_pair():
    return [(r, r ^ 1) for r in range(ROWS)]


def row_shift(d):
    return [(r, (r + d) % ROWS) for r in range(ROWS)]


def body(
    source_coords,
    target_coords,
    source_order,
    target_order,
    source_mass,
    target_mass,
    target_potential,
    tile_source,
    tile_target,
    tile_count,
):
    shape = jax.ShapeDtypeStruct
    y = lax.rem(lax.axis_index("col"), Y)
    mass = source_mass.reshape(SRC // 128, 128)

    pack = call(
        target_kernel,
        "target_gather",
        shape((PACK, TGT), f32),
        [anywhere()] * 5 + [smem()],
        [
            pltpu.VMEM((48, TGT), bf16),
            pltpu.VMEM((PC, TGT), bf16),
            pltpu.VMEM((1, TGT), jnp.int32),
            pltpu.VMEM((1, TGT), f32),
            pltpu.VMEM((1, CAP), jnp.int32),
            pltpu.VMEM((1, CAP), jnp.int32),
            pltpu.SemaphoreType.DMA((5,)),
        ],
        flops=2 * 48 * TGT * TGT,
        limit=60,
    )(
        target_coords,
        target_order,
        target_potential.reshape(1, TGT),
        tile_source.reshape(1, CAP),
        tile_target.reshape(1, CAP),
        tile_count,
    )
    packs = [pack] + [lax.ppermute(pack, "col", y_shift(d)) for d in range(1, Y)]

    source = call(
        gather_kernel,
        "source_gather",
        shape((CHUNK, 128), bf16),
        [anywhere()] * 3,
        [
            pltpu.VMEM((SRC, 128), f32),
            pltpu.VMEM((BLK, 128), f32),
            pltpu.VMEM((PC, SRC), bf16),
            pltpu.VMEM((SRC // 128, 128), f32),
            pltpu.SMEM((1, CHUNK), jnp.int32),
            pltpu.VMEM((CHUNK, 128), bf16),
            pltpu.SemaphoreType.DMA((LOADS,)),
            pltpu.SemaphoreType.DMA((2,)),
            pltpu.SemaphoreType.DMA((STORES,)),
        ],
        flops=2 * 10**10,
        nbytes=64 * 2**20,
        limit=56,
        out_specs=anywhere(),
    )(source_coords, mass, source_order)

    lists = jnp.concatenate([lax.dynamic_slice(p, (PACK - 1, y * CAP), (1, CAP)) for p in packs], axis=0)
    codes = lists.astype(jnp.int32) - 1
    counts = jnp.sum((lists > 0.5).astype(jnp.int32), axis=1)

    partial, late = call(
        row_kernel,
        "row_pass",
        [shape((2 * NB, 128), f32), shape((Y * TGT, 128), bf16)],
        [anywhere()] + [vmem()] * 4 + [smem()] * 2,
        [
            pltpu.VMEM((CHUNK, 128), bf16),
            pltpu.VMEM((Y * TGT, 128), bf16),
            pltpu.VMEM((Y * TGT, 128), bf16),
            pltpu.VMEM((2 * NB, 128), f32),
            pltpu.VMEM((2 * NB, 128), f32),
            pltpu.SMEM((Y * CAP,), jnp.int32),
            pltpu.SemaphoreType.DMA((2,)),
        ],
        out_specs=[vmem(), anywhere()],
    )(source, *packs, codes, counts)

    partials = [partial] + [lax.ppermute(partial, "col", z_shift(d)) for d in (2, 4, 6)]
    lse = call(merge_kernel, "row_merge_four", shape((2 * NB, 128), f32), [vmem()] * 4, [])(*partials)
    partials = [lse, lax.ppermute(lse, "col", z_pair())]
    lse = call(merge_kernel, "row_merge_two", shape((2 * NB, 128), f32), [vmem()] * 2, [])(*partials)
    lses = [lse] + [lax.ppermute(lse, "col", y_shift(d)) for d in range(1, Y)]

    target_partial = call(
        col_kernel,
        "col_pass",
        shape((2 * Y * TB, 128), f32),
        [anywhere(), anywhere(), vmem()] + [smem()] * 2,
        [
            pltpu.VMEM((CHUNK, 128), bf16),
            pltpu.VMEM((Y * TGT, 128), bf16),
            pltpu.VMEM((2 * Y * TB, 128), f32),
            pltpu.VMEM((2 * Y * TB, 128), f32),
            pltpu.SMEM((Y * CAP,), jnp.int32),
            pltpu.SemaphoreType.DMA((LOADS + 1,)),
        ],
        flops=2 * 10**10,
        exps=10**7,
    )(source, late, lse, codes, counts)

    order_rows = source_order.reshape(SRC // 128, 128)
    cost = dict(flops=2 * 512 * 256 * CHUNK, nbytes=2**20)
    totals = shape((512, 256), f32)
    keep = [pltpu.VMEM((512, 256), f32)]

    def piece(d, before=None):
        chunk = lax.rem(y + Y - d, Y).reshape(1)
        kernel = functools.partial(scatter_kernel, before is None, None)
        return call(
            kernel, f"source_scatter_{d}", totals, [vmem()] * 2 + [smem()] + [vmem()] * (before is not None), keep, **cost
        )(order_rows, lses[d], chunk, *([] if before is None else [before]))

    own = [target_partial[0 : 2 * TB]] + [
        lax.ppermute(target_partial[2 * d * TB : 2 * (d + 1) * TB], "col", y_shift(-d)) for d in range(1, Y)
    ]
    scattered = piece(0)
    own, scattered = lax.optimization_barrier((own, scattered))
    merge = lambda name, parts: call(merge_kernel, name, shape((2 * TB, 128), f32), [vmem()] * len(parts), [])(*parts)
    own = merge("col_merge_y", own)
    own = [own, lax.ppermute(own, "row", row_pair())]
    scattered = piece(1, scattered)
    own, scattered = lax.optimization_barrier((own, scattered))
    own = merge("col_merge_core", own)
    own = [own] + [lax.ppermute(own, "row", row_shift(d)) for d in (2, 4, 6)]
    scattered = piece(2, scattered)
    source_update = call(
        last_scatter_kernel,
        "source_scatter_3",
        shape((SRC // 128, 128), f32),
        [vmem()] * 3 + [smem(), vmem()],
        keep,
        **cost,
    )(mass, order_rows, lses[3], lax.rem(y + Y - 3, Y).reshape(1), scattered)
    own, source_update = lax.optimization_barrier((own, source_update))
    target_update = call(
        final_kernel,
        "target_scatter",
        shape((TGT // 128, 128), f32),
        [vmem()] * 7,
        [],
    )(
        *own,
        target_order.reshape(TGT // 128, 128),
        target_mass.reshape(TGT // 128, 128),
        target_potential.reshape(TGT // 128, 128),
    )
    return (source_update.reshape(SRC), target_update.reshape(TGT))


def solution(mesh):
    in_specs = (
        P(None, "row"),
        P(None, "col"),
        P("row", None),
        P("col", None),
        P("row"),
        P("col"),
        P("col"),
        P("row", "col", None),
        P("row", "col", None),
        P("row", "col"),
    )
    out_specs = (P("row"), P("col"))
    return jax.shard_map(body, mesh=mesh, in_specs=in_specs, out_specs=out_specs, check_vma=False)
```

```python
import functools
import math

import jax
import jax.numpy as jnp
from jax import lax
from jax.experimental import pallas as pl
from jax.experimental.pallas import tpu as pltpu
from jax.sharding import PartitionSpec as P

PC = 32
BLK = 256
Z = 8
Y = 4
ROWS = 8
SRC = 65536
TGT = 2048
CHUNK = SRC // Y
NB = CHUNK // BLK
TB = TGT // BLK
CAP = 256
UNROLL = 16
SCATTER = 8
BUILD = 32
LOADS = 4
STORES = 4
PACK = 40
LOG2E = math.log2(math.e)
KAPPA = 10.0 * LOG2E
LN2 = math.log(2.0)
LOW = -1e30

f32 = jnp.float32
bf16 = jnp.bfloat16
NT = (((1,), (1,)), ((), ()))


def iota(shape, axis):
    return lax.broadcasted_iota(jnp.int32, shape, axis)


def indicator(condition):
    return jnp.where(condition, 1.0, 0.0).astype(bf16)


def three(value):
    first = value.astype(bf16).astype(f32)
    rest = value - first
    second = rest.astype(bf16).astype(f32)
    return first, second, rest - second


def vmem():
    return pl.BlockSpec(memory_space=pltpu.VMEM)


def anywhere():
    return pl.BlockSpec(memory_space=pl.ANY)


def smem():
    return pl.BlockSpec(memory_space=pltpu.SMEM)


def call(kernel, name, out_shape, in_specs, scratch, flops=0, nbytes=0, exps=0, limit=48, out_specs=None):
    many = isinstance(out_shape, (list, tuple))
    return pl.pallas_call(
        kernel,
        out_shape=out_shape,
        in_specs=in_specs,
        out_specs=out_specs or ([vmem() for _ in out_shape] if many else vmem()),
        scratch_shapes=scratch,
        compiler_params=pltpu.CompilerParams(vmem_limit_bytes=limit * 2**20),
        cost_estimate=pl.CostEstimate(flops=flops, bytes_accessed=nbytes, transcendentals=exps),
        name=name,
    )


def target_kernel(*refs):
    given, count, out, left, held, sems = refs[:5], refs[5], refs[6], refs[7], refs[8:13], refs[13]
    loads = [pltpu.make_async_copy(here, there, sems.at[k]) for k, (here, there) in enumerate(zip(given, held))]
    for load in loads:
        load.start()
    for load in loads:
        load.wait()
    coords, order, potential, which_source, which_target = held
    sub8 = iota((8, TGT), 0)
    vh, vm, vl = three(jnp.broadcast_to(potential[...], (8, TGT)))
    part = jnp.where(sub8 == 0, vh, jnp.where(sub8 == 1, vm, jnp.where(sub8 == 2, vl, 0.0)))
    left[0:32, :] = coords[...]
    left[32:48, :] = jnp.concatenate([part, jnp.zeros((8, TGT), f32)], axis=0).astype(bf16)
    number = iota((TGT, BLK), 0)

    def one_block(b, carry):
        span = pl.ds(pl.multiple_of(b * BLK, BLK), BLK)
        picked = indicator(number == order[:, span])
        got = jnp.dot(left[...], picked, preferred_element_type=f32)
        y = got[0:32]
        v = got[32:33] + got[33:34] + got[34:35]
        a = (v - jnp.sum(y * y, axis=0, keepdims=True) * (1.0 / PC)) * KAPPA
        out[0:32, span] = y
        out[32:40, span] = jnp.broadcast_to(a, (8, BLK))
        return carry

    lax.fori_loop(0, TB, one_block, 0)

    src = which_source[...]
    used = iota((1, CAP), 1) < count[0, 0]
    quarter = jnp.where(used, src // NB, 7)
    member = jnp.where(iota((8, CAP), 0) == quarter, 1.0, 0.0)
    earlier = indicator(iota((CAP, CAP), 0) < iota((CAP, CAP), 1))
    before = jnp.dot(member.astype(bf16), earlier, preferred_element_type=f32)
    rank = jnp.sum(member * before, axis=0, keepdims=True).astype(jnp.int32)
    place = quarter * CAP + rank
    sub16 = iota((16, CAP), 0)
    code = jnp.where(
        sub16 == 0,
        ((src % NB) * 8).astype(f32),
        jnp.where(sub16 == 1, (which_target[...] + 1).astype(f32), 0.0),
    ).astype(bf16)
    chosen = indicator(iota((Y * CAP, CAP), 0) == place)
    listed = lax.dot_general(code, chosen, NT, preferred_element_type=f32)
    out[39:40, 0 : Y * CAP] = listed[0:1] + listed[1:2]
    out[39:40, Y * CAP :] = jnp.zeros((1, TGT - Y * CAP), f32)


def gather_kernel(coords_all, mass_all, order_all, out_all, table, rows, coords, mass, order, out, sems, in_sem, out_sem):
    start = pl.multiple_of(lax.rem(lax.axis_index("col"), Y) * CHUNK, CHUNK)
    share = SRC // LOADS
    weights = pltpu.make_async_copy(mass_all, mass, in_sem.at[0])
    listed = pltpu.make_async_copy(order_all.at[:, pl.ds(start, CHUNK)], order, in_sem.at[1])
    loads = [
        pltpu.make_async_copy(
            coords_all.at[:, k * share : (k + 1) * share], coords.at[:, k * share : (k + 1) * share], sems.at[k]
        )
        for k in range(LOADS)
    ]
    weights.start()
    for load in loads:
        load.start()
    listed.start()
    sub8 = iota((8, 128), 0)
    lane = lax.rem(sub8, 4)
    first = jnp.where(sub8 == 0, 1.0, 0.0)
    blank = jnp.zeros((16, 128), bf16)

    def build(b):
        span = pl.ds(pl.multiple_of(b * 128, 128), 128)
        x = coords[:, span]
        wide = x.astype(f32)
        norm = jnp.sum(wide * wide, axis=0, keepdims=True) * (-KAPPA / PC)
        weight = mass[pl.ds(b, 1), :] * LOG2E
        both = jnp.where(sub8 < 4, jnp.broadcast_to(norm, (8, 128)), jnp.broadcast_to(weight, (8, 128)))
        h, m, l = three(both)
        part = jnp.where(lane == 0, h, jnp.where(lane == 1, m, jnp.where(lane == 2, l, 1.0)))
        part = jnp.concatenate([part, first], axis=0).astype(bf16)
        table[span, :] = jnp.concatenate([x, x, x, part, blank], axis=0).T.astype(f32)

    weights.wait()
    for k in range(LOADS):
        loads[k].wait()

        def several(g, carry):
            for u in range(BUILD):
                build(k * (share // 128) + g * BUILD + u)
            return carry

        lax.fori_loop(0, share // 128 // BUILD, several, 0)

    listed.wait()

    def one_block(b, carry):
        base = b * BLK
        for i in range(BLK):
            rows[pl.ds(i, 1), :] = table[pl.ds(order[0, base + i], 1), :]
        out[pl.ds(pl.multiple_of(base, BLK), BLK), :] = rows[...].astype(bf16)
        return carry

    share = CHUNK // STORES
    stores = []
    for k in range(STORES):
        lax.fori_loop(k * (NB // STORES), (k + 1) * (NB // STORES), one_block, 0)
        here = slice(k * share, (k + 1) * share)
        stores.append(pltpu.make_async_copy(out.at[here, :], out_all.at[here, :], out_sem.at[k]))
        stores[-1].start()
    for store in stores:
        store.wait()


def tiles(left_of, right_of, slot_of, highest, total, counts, codes, entries):
    filled = 0
    for d in range(Y):

        def copy(e, base):
            code = codes[d, e]
            entries[base + e] = code + (code // 8) * (TB * (Y - 1)) + d * TB
            return base

        lax.fori_loop(0, counts[d], copy, filled)
        filled = filled + counts[d]

    def tile(e):
        code = entries[e]
        s, t = code // (Y * TB), lax.rem(code, Y * TB)
        left = left_of(s, t)
        found = []
        for half in range(2):
            score = lax.dot_general(left, right_of(s, t, half), NT, preferred_element_type=f32)
            top = jnp.max(score, axis=0, keepdims=True)
            found.append((top, jnp.sum(jnp.exp2(score - top), axis=0, keepdims=True)))
        return slot_of(s, t), found

    def add(slot, found, has):
        for half, (top, summed) in enumerate(found):
            here = pl.ds(2 * slot + half, 1)
            top = jnp.where(has, top, LOW)
            old = highest[here, :]
            new = jnp.maximum(old, top)
            summed = jnp.where(has, summed, 0.0)
            total[here, :] = total[here, :] * jnp.exp2(old - new) + summed * jnp.exp2(top - new)
            highest[here, :] = new

    highest[...] = jnp.full(highest.shape, LOW, f32)
    total[...] = jnp.zeros(total.shape, f32)

    def several(g, carry):
        found = [tile(jnp.minimum(g * UNROLL + u, filled - 1)) for u in range(UNROLL)]
        for u in range(UNROLL):
            add(*found[u], g * UNROLL + u < filled)
        return carry

    lax.fori_loop(0, (filled + UNROLL - 1) // UNROLL, several, 0)
    return jnp.where(total[...] > 0.0, highest[...] + jnp.log2(total[...]), LOW)


def row_kernel(
    source_all, p0, p1, p2, p3, codes, counts, partial, late_all, source, late, early, highest, total, entries, sem
):
    load = pltpu.make_async_copy(source_all, source, sem.at[0])
    load.start()
    lane = iota((128, 128), 1)
    turned = indicator(((lane >= 100) & (lane <= 102)) | ((lane >= 105) & (lane <= 107)))
    sub8 = iota((8, 128), 0)
    for d, pack in enumerate((p0, p1, p2, p3)):

        def build(b, carry):
            span = pl.ds(pl.multiple_of(b * 128, 128), 128)
            h, m, l = three(pack[0:32, span] * (KAPPA / 16.0))
            ah, am, al = three(jnp.broadcast_to(pack[32:33, span], (8, 128)))
            part = jnp.where(sub8 < 3, 1.0, jnp.where(sub8 == 3, ah, jnp.where(sub8 == 7, am, 0.0)))
            last = jnp.where(sub8 == 0, al, 0.0)
            rows = jnp.concatenate([h, m, l, part, last, jnp.zeros((16, 128), f32)], axis=0).astype(bf16).T
            place = pl.ds(pl.multiple_of(d * TGT + b * 128, 128), 128)
            early[place, :] = rows
            late[place, :] = rows + turned
            return carry

        lax.fori_loop(0, TGT // 128, build, 0)

    store = pltpu.make_async_copy(late, late_all, sem.at[1])
    store.start()
    load.wait()
    partial[...] = tiles(
        lambda s, t: early[pl.ds(pl.multiple_of(t * BLK, BLK), BLK), :],
        lambda s, t, half: source[pl.ds(pl.multiple_of(s * BLK + half * 128, 128), 128), :],
        lambda s, t: s,
        highest,
        total,
        counts,
        codes,
        entries,
    )
    store.wait()


def merged(parts):
    top = functools.reduce(jnp.maximum, parts)
    return top + jnp.log2(sum(jnp.exp2(part - top) for part in parts))


def merge_kernel(*refs):
    refs[-1][...] = merged([ref[...] for ref in refs[:-1]])


def col_kernel(source_all, late_all, lse, codes, counts, partial, filled, late, highest, total, entries, sems):
    share = CHUNK // LOADS
    second = pltpu.make_async_copy(late_all, late, sems.at[LOADS])
    loads = []
    for k in range(LOADS):
        here = slice(k * share, (k + 1) * share)
        loads.append(pltpu.make_async_copy(source_all.at[here, :], filled.at[here, :], sems.at[k]))
        loads[-1].start()
    second.start()
    sub8 = iota((8, 128), 0)

    def fill(g, carry):
        for u in range(4):
            row = -lse[pl.ds(g * 4 + u, 1), :]
            h, m, l = three(jnp.broadcast_to(row, (8, 128)))
            part = jnp.where(sub8 == 1, h, jnp.where(sub8 == 2, m, jnp.where(sub8 == 3, l, 0.0)))
            rows = jnp.concatenate([jnp.zeros((104, 128), f32), part, jnp.zeros((16, 128), f32)], axis=0)
            span = pl.ds(pl.multiple_of((g * 4 + u) * 128, 128), 128)
            filled[span, :] = filled[span, :] + rows.astype(bf16).T
        return carry

    for k in range(LOADS):
        loads[k].wait()
        lax.fori_loop(k * (share // 512), (k + 1) * (share // 512), fill, 0)
    second.wait()
    partial[...] = tiles(
        lambda s, t: filled[pl.ds(pl.multiple_of(s * BLK, BLK), BLK), :],
        lambda s, t, half: late[pl.ds(pl.multiple_of(t * BLK + half * 128, 128), 128), :],
        lambda s, t: t,
        highest,
        total,
        counts,
        codes,
        entries,
    )


def flat(block):
    return jnp.concatenate([block[u : u + 1, :] for u in range(8)], axis=1)


def spread(order_row, value_row, high_rows):
    n = order_row.shape[1]
    high = indicator(iota((high_rows, n), 0) == order_row // 128)
    match = iota((128, n), 0) == lax.rem(order_row, 128)
    first = value_row.astype(bf16).astype(f32)
    low = jnp.concatenate(
        [jnp.where(match, first, 0.0), jnp.where(match, value_row - first, 0.0)], axis=0
    ).astype(bf16)
    return lax.dot_general(high, low, NT, preferred_element_type=f32)


def scatter_kernel(mass, order, first_lse, second_lse, chunk, *refs):
    half = lax.rem(lax.axis_index("col") // Y, 2)
    out, total = refs[-2:]
    number = iota((256, 1024), 0).astype(f32).astype(bf16)
    one, zero = jnp.ones((), bf16), jnp.zeros((), bf16)
    if mass is None:
        total[...] = jnp.zeros(total.shape, f32)
    else:
        total[...] = refs[0][...]
    for k, lse in enumerate((first_lse, second_lse)):
        first = chunk[k] * (2 * NB)

        def product(g):
            cell = flat(order[pl.ds(pl.multiple_of(first + g * 8, 8), 8), :])
            value = flat(lse[pl.ds(pl.multiple_of(g * 8, 8), 8), :])
            column = lax.rem(cell // 128, 256).astype(f32).astype(bf16)
            row = ((cell // (SRC // 2) - half) * 128 + lax.rem(cell, 128)).astype(f32).astype(bf16)
            big = value.astype(bf16)
            small = (value - big.astype(f32)).astype(bf16)
            match = number[0:128] == row
            left = jnp.concatenate([jnp.where(match, big, zero), jnp.where(match, small, zero)], axis=0)
            right = jnp.where(number == column, one, zero)
            return lax.dot_general(left, right, NT, preferred_element_type=f32)

        def step(g, carry):
            total[...] += sum(product(g * SCATTER + u) for u in range(SCATTER))
            return carry

        lax.fori_loop(0, NB // 4 // SCATTER, step, 0)
    if mass is None:
        out[...] = total[...]
        return
    base = half * 256
    for side in range(2):
        here = slice(side * 128, side * 128 + 128)
        both = total[0:128, here] + total[128:256, here]
        weight = mass[pl.ds(pl.multiple_of(base + side * 128, 128), 128), :]
        out[here, :] = 0.1 * weight - (0.1 * LN2) * both.T


def last_scatter_kernel(mass, *refs):
    scatter_kernel(mass, *refs)


def final_kernel(*refs):
    order, mass, potential, own, other, source_out, out = refs[4:]
    half = lax.rem(lax.axis_index("col") // Y, 2)
    source_out[pl.ds(pl.multiple_of(half * 256, 256), 256), :] = own[...]
    source_out[pl.ds(pl.multiple_of(256 - half * 256, 256), 256), :] = other[...]
    lse = merged([ref[...] for ref in refs[:4]])
    total = jnp.zeros((TGT // 128, 256), f32)
    for g in range(TGT // 1024):
        total += spread(flat(order[g * 8 : g * 8 + 8, :]), flat(lse[g * 8 : g * 8 + 8, :]), TGT // 128)
    out[...] = 0.1 * mass[...] + potential[...] - (0.1 * LN2) * (total[:, 0:128] + total[:, 128:256])


def y_shift(d):
    return [(z * Y + y, z * Y + (y + d) % Y) for z in range(Z) for y in range(Y)]


def z_shift(d):
    return [(z * Y + y, (z + d) % Z * Y + y) for z in range(Z) for y in range(Y)]


def z_pair():
    return [(z * Y + y, (z ^ 1) * Y + y) for z in range(Z) for y in range(Y)]


def row_pair():
    return [(r, r ^ 1) for r in range(ROWS)]


def row_shift(d):
    return [(r, (r + d) % ROWS) for r in range(ROWS)]


def body(
    source_coords,
    target_coords,
    source_order,
    target_order,
    source_mass,
    target_mass,
    target_potential,
    tile_source,
    tile_target,
    tile_count,
):
    shape = jax.ShapeDtypeStruct
    y = lax.rem(lax.axis_index("col"), Y)
    mass = source_mass.reshape(SRC // 128, 128)

    pack = call(
        target_kernel,
        "target_gather",
        shape((PACK, TGT), f32),
        [anywhere()] * 5 + [smem()],
        [
            pltpu.VMEM((48, TGT), bf16),
            pltpu.VMEM((PC, TGT), bf16),
            pltpu.VMEM((1, TGT), jnp.int32),
            pltpu.VMEM((1, TGT), f32),
            pltpu.VMEM((1, CAP), jnp.int32),
            pltpu.VMEM((1, CAP), jnp.int32),
            pltpu.SemaphoreType.DMA((5,)),
        ],
        flops=2 * 48 * TGT * TGT,
        limit=60,
    )(
        target_coords,
        target_order,
        target_potential.reshape(1, TGT),
        tile_source.reshape(1, CAP),
        tile_target.reshape(1, CAP),
        tile_count,
    )
    packs = [pack] + [lax.ppermute(pack, "col", y_shift(d)) for d in range(1, Y)]

    source = call(
        gather_kernel,
        "source_gather",
        shape((CHUNK, 128), bf16),
        [anywhere()] * 3,
        [
            pltpu.VMEM((SRC, 128), f32),
            pltpu.VMEM((BLK, 128), f32),
            pltpu.VMEM((PC, SRC), bf16),
            pltpu.VMEM((SRC // 128, 128), f32),
            pltpu.SMEM((1, CHUNK), jnp.int32),
            pltpu.VMEM((CHUNK, 128), bf16),
            pltpu.SemaphoreType.DMA((LOADS,)),
            pltpu.SemaphoreType.DMA((2,)),
            pltpu.SemaphoreType.DMA((STORES,)),
        ],
        flops=2 * 10**10,
        nbytes=64 * 2**20,
        limit=56,
        out_specs=anywhere(),
    )(source_coords, mass, source_order)

    lists = jnp.concatenate([lax.dynamic_slice(p, (PACK - 1, y * CAP), (1, CAP)) for p in packs], axis=0)
    codes = lists.astype(jnp.int32) - 1
    counts = jnp.sum((lists > 0.5).astype(jnp.int32), axis=1)

    partial, late = call(
        row_kernel,
        "row_pass",
        [shape((2 * NB, 128), f32), shape((Y * TGT, 128), bf16)],
        [anywhere()] + [vmem()] * 4 + [smem()] * 2,
        [
            pltpu.VMEM((CHUNK, 128), bf16),
            pltpu.VMEM((Y * TGT, 128), bf16),
            pltpu.VMEM((Y * TGT, 128), bf16),
            pltpu.VMEM((2 * NB, 128), f32),
            pltpu.VMEM((2 * NB, 128), f32),
            pltpu.SMEM((Y * CAP,), jnp.int32),
            pltpu.SemaphoreType.DMA((2,)),
        ],
        out_specs=[vmem(), anywhere()],
    )(source, *packs, codes, counts)

    partials = [partial] + [lax.ppermute(partial, "col", z_shift(d)) for d in (2, 4, 6)]
    lse = call(merge_kernel, "row_merge_four", shape((2 * NB, 128), f32), [vmem()] * 4, [])(*partials)
    partials = [lse, lax.ppermute(lse, "col", z_pair())]
    lse = call(merge_kernel, "row_merge_two", shape((2 * NB, 128), f32), [vmem()] * 2, [])(*partials)
    lses = [lse] + [lax.ppermute(lse, "col", y_shift(d)) for d in range(1, Y)]

    target_partial = call(
        col_kernel,
        "col_pass",
        shape((2 * Y * TB, 128), f32),
        [anywhere(), anywhere(), vmem()] + [smem()] * 2,
        [
            pltpu.VMEM((CHUNK, 128), bf16),
            pltpu.VMEM((Y * TGT, 128), bf16),
            pltpu.VMEM((2 * Y * TB, 128), f32),
            pltpu.VMEM((2 * Y * TB, 128), f32),
            pltpu.SMEM((Y * CAP,), jnp.int32),
            pltpu.SemaphoreType.DMA((LOADS + 1,)),
        ],
        flops=2 * 10**10,
        exps=10**7,
    )(source, late, lse, codes, counts)

    order_rows = source_order.reshape(SRC // 128, 128)
    cost = dict(flops=2 * 512 * 256 * CHUNK, nbytes=2**20)
    keep = [pltpu.VMEM((256, 256), f32)]
    chunks = lax.rem(y + Y - jnp.arange(Y, dtype=jnp.int32), Y)

    def merge(name, parts):
        return call(merge_kernel, name, shape((2 * TB, 128), f32), [vmem()] * len(parts), [])(*parts)

    own = [target_partial[0 : 2 * TB]] + [
        lax.ppermute(target_partial[2 * d * TB : 2 * (d + 1) * TB], "col", y_shift(-d)) for d in range(1, Y)
    ]
    scattered = call(
        functools.partial(scatter_kernel, None),
        "source_scatter_0",
        shape((256, 256), f32),
        [vmem()] * 3 + [smem()],
        keep,
        **cost,
    )(order_rows, lses[0], lses[1], chunks[0:2])
    own, scattered = lax.optimization_barrier((own, scattered))
    own = merge("col_merge_y", own)
    own = [own, lax.ppermute(own, "row", row_pair())]
    mine = call(
        last_scatter_kernel,
        "source_scatter_1",
        shape((SRC // 256, 128), f32),
        [vmem()] * 4 + [smem(), vmem()],
        keep,
        **cost,
    )(mass, order_rows, lses[2], lses[3], chunks[2:4], scattered)
    own, mine = lax.optimization_barrier((own, mine))
    other = lax.ppermute(mine, "col", z_pair())
    own = merge("col_merge_core", own)
    own = [own] + [lax.ppermute(own, "row", row_shift(d)) for d in (2, 4, 6)]
    source_update, target_update = call(
        final_kernel,
        "target_scatter",
        [shape((SRC // 128, 128), f32), shape((TGT // 128, 128), f32)],
        [vmem()] * 9,
        [],
    )(
        *own,
        target_order.reshape(TGT // 128, 128),
        target_mass.reshape(TGT // 128, 128),
        target_potential.reshape(TGT // 128, 128),
        mine,
        other,
    )
    return (source_update.reshape(SRC), target_update.reshape(TGT))


def solution(mesh):
    in_specs = (
        P(None, "row"),
        P(None, "col"),
        P("row", None),
        P("col", None),
        P("row"),
        P("col"),
        P("col"),
        P("row", "col", None),
        P("row", "col", None),
        P("row", "col"),
    )
    out_specs = (P("row"), P("col"))
    return jax.shard_map(body, mesh=mesh, in_specs=in_specs, out_specs=out_specs, check_vma=False)
```

```python
import functools
import math

import jax
import jax.numpy as jnp
from jax import lax
from jax.experimental import pallas as pl
from jax.experimental.pallas import tpu as pltpu
from jax.sharding import PartitionSpec as P

PC = 32
BLK = 256
Z = 8
Y = 4
ROWS = 8
SRC = 65536
TGT = 2048
CHUNK = SRC // Y
NB = CHUNK // BLK
TB = TGT // BLK
CAP = 256
UNROLL = 16
SCATTER = 16
BUILD = 64
FILL = 32
LOADS = 4
STORES = 4
PACK = 40
LOG2E = math.log2(math.e)
KAPPA = 10.0 * LOG2E
LN2 = math.log(2.0)
LOW = -1e30

f32 = jnp.float32
bf16 = jnp.bfloat16
NT = (((1,), (1,)), ((), ()))


def iota(shape, axis):
    return lax.broadcasted_iota(jnp.int32, shape, axis)


def indicator(condition):
    return jnp.where(condition, 1.0, 0.0).astype(bf16)


def three(value):
    first = value.astype(bf16).astype(f32)
    rest = value - first
    second = rest.astype(bf16).astype(f32)
    return first, second, rest - second


def vmem():
    return pl.BlockSpec(memory_space=pltpu.VMEM)


def anywhere():
    return pl.BlockSpec(memory_space=pl.ANY)


def smem():
    return pl.BlockSpec(memory_space=pltpu.SMEM)


def call(kernel, name, out_shape, in_specs, scratch, flops=0, nbytes=0, exps=0, limit=48, out_specs=None):
    many = isinstance(out_shape, (list, tuple))
    return pl.pallas_call(
        kernel,
        out_shape=out_shape,
        in_specs=in_specs,
        out_specs=out_specs or ([vmem() for _ in out_shape] if many else vmem()),
        scratch_shapes=scratch,
        compiler_params=pltpu.CompilerParams(vmem_limit_bytes=limit * 2**20),
        cost_estimate=pl.CostEstimate(flops=flops, bytes_accessed=nbytes, transcendentals=exps),
        name=name,
    )


def target_kernel(*refs):
    given, count, out, left, held, sems = refs[:5], refs[5], refs[6], refs[7], refs[8:13], refs[13]
    loads = [pltpu.make_async_copy(here, there, sems.at[k]) for k, (here, there) in enumerate(zip(given, held))]
    for load in loads:
        load.start()
    for load in loads:
        load.wait()
    coords, order, potential, which_source, which_target = held
    sub8 = iota((8, TGT), 0)
    vh, vm, vl = three(jnp.broadcast_to(potential[...], (8, TGT)))
    part = jnp.where(sub8 == 0, vh, jnp.where(sub8 == 1, vm, jnp.where(sub8 == 2, vl, 0.0)))
    left[0:32, :] = coords[...]
    left[32:48, :] = jnp.concatenate([part, jnp.zeros((8, TGT), f32)], axis=0).astype(bf16)
    number = iota((TGT, BLK), 0)

    def one_block(b):
        span = pl.ds(pl.multiple_of(b * BLK, BLK), BLK)
        picked = indicator(number == order[:, span])
        got = jnp.dot(left[...], picked, preferred_element_type=f32)
        y = got[0:32]
        v = got[32:33] + got[33:34] + got[34:35]
        a = (v - jnp.sum(y * y, axis=0, keepdims=True) * (1.0 / PC)) * KAPPA
        out[0:32, span] = y
        out[32:40, span] = jnp.broadcast_to(a, (8, BLK))

    def two_blocks(g, carry):
        one_block(2 * g)
        one_block(2 * g + 1)
        return carry

    lax.fori_loop(0, TB // 2, two_blocks, 0)

    src = which_source[...]
    used = iota((1, CAP), 1) < count[0, 0]
    quarter = jnp.where(used, src // NB, 7)
    member = jnp.where(iota((8, CAP), 0) == quarter, 1.0, 0.0)
    earlier = indicator(iota((CAP, CAP), 0) < iota((CAP, CAP), 1))
    before = jnp.dot(member.astype(bf16), earlier, preferred_element_type=f32)
    rank = jnp.sum(member * before, axis=0, keepdims=True).astype(jnp.int32)
    place = quarter * CAP + rank
    sub16 = iota((16, CAP), 0)
    code = jnp.where(
        sub16 == 0,
        ((src % NB) * 8).astype(f32),
        jnp.where(sub16 == 1, (which_target[...] + 1).astype(f32), 0.0),
    ).astype(bf16)
    chosen = indicator(iota((Y * CAP, CAP), 0) == place)
    listed = lax.dot_general(code, chosen, NT, preferred_element_type=f32)
    out[39:40, 0 : Y * CAP] = listed[0:1] + listed[1:2]
    out[39:40, Y * CAP :] = jnp.zeros((1, TGT - Y * CAP), f32)


def gather_kernel(coords_all, mass_all, order_all, out_all, table, rows, coords, mass, order, out, sems, in_sem, out_sem):
    start = pl.multiple_of(lax.rem(lax.axis_index("col"), Y) * CHUNK, CHUNK)
    share = SRC // LOADS
    weights = pltpu.make_async_copy(mass_all, mass, in_sem.at[0])
    listed = pltpu.make_async_copy(order_all.at[:, pl.ds(start, CHUNK)], order, in_sem.at[1])
    loads = [
        pltpu.make_async_copy(
            coords_all.at[:, k * share : (k + 1) * share], coords.at[:, k * share : (k + 1) * share], sems.at[k]
        )
        for k in range(LOADS)
    ]
    weights.start()
    for load in loads:
        load.start()
    listed.start()
    sub8 = iota((8, 128), 0)
    lane = lax.rem(sub8, 4)
    first = jnp.where(sub8 == 0, 1.0, 0.0)
    blank = jnp.zeros((16, 128), bf16)

    def build(b):
        span = pl.ds(pl.multiple_of(b * 128, 128), 128)
        x = coords[:, span]
        wide = x.astype(f32)
        norm = jnp.sum(wide * wide, axis=0, keepdims=True) * (-KAPPA / PC)
        weight = mass[pl.ds(b, 1), :] * LOG2E
        both = jnp.where(sub8 < 4, jnp.broadcast_to(norm, (8, 128)), jnp.broadcast_to(weight, (8, 128)))
        h, m, l = three(both)
        part = jnp.where(lane == 0, h, jnp.where(lane == 1, m, jnp.where(lane == 2, l, 1.0)))
        part = jnp.concatenate([part, first], axis=0).astype(bf16)
        table[span, :] = jnp.concatenate([x, x, x, part, blank], axis=0).T.astype(f32)

    weights.wait()
    for k in range(LOADS):
        loads[k].wait()

        def several(g, carry):
            for u in range(BUILD):
                build(k * (share // 128) + g * BUILD + u)
            return carry

        lax.fori_loop(0, share // 128 // BUILD, several, 0)

    listed.wait()

    def one_block(b, carry):
        base = b * BLK
        for i in range(BLK):
            rows[pl.ds(i, 1), :] = table[pl.ds(order[0, base + i], 1), :]
        out[pl.ds(pl.multiple_of(base, BLK), BLK), :] = rows[...].astype(bf16)
        return carry

    share = CHUNK // STORES
    stores = []
    for k in range(STORES):
        lax.fori_loop(k * (NB // STORES), (k + 1) * (NB // STORES), one_block, 0)
        here = slice(k * share, (k + 1) * share)
        stores.append(pltpu.make_async_copy(out.at[here, :], out_all.at[here, :], out_sem.at[k]))
        stores[-1].start()
    for store in stores:
        store.wait()


def tiles(left_of, right_of, slot_of, highest, total, counts, codes, entries):
    filled = 0
    for d in range(Y):

        def copy(e, base):
            code = codes[d, e]
            entries[base + e] = code + (code // 8) * (TB * (Y - 1)) + d * TB
            return base

        lax.fori_loop(0, counts[d], copy, filled)
        filled = filled + counts[d]

    def tile(e):
        code = entries[e]
        s, t = code // (Y * TB), lax.rem(code, Y * TB)
        left = left_of(s, t)
        found = []
        for half in range(2):
            score = lax.dot_general(left, right_of(s, t, half), NT, preferred_element_type=f32)
            top = jnp.max(score, axis=0, keepdims=True)
            found.append((top, jnp.sum(jnp.exp2(score - top), axis=0, keepdims=True)))
        return slot_of(s, t), found

    def add(slot, found, has):
        for half, (top, summed) in enumerate(found):
            here = pl.ds(2 * slot + half, 1)
            top = jnp.where(has, top, LOW)
            old = highest[here, :]
            new = jnp.maximum(old, top)
            summed = jnp.where(has, summed, 0.0)
            total[here, :] = total[here, :] * jnp.exp2(old - new) + summed * jnp.exp2(top - new)
            highest[here, :] = new

    highest[...] = jnp.full(highest.shape, LOW, f32)
    total[...] = jnp.zeros(total.shape, f32)

    def several(g, carry):
        found = [tile(jnp.minimum(g * UNROLL + u, filled - 1)) for u in range(UNROLL)]
        for u in range(UNROLL):
            add(*found[u], g * UNROLL + u < filled)
        return carry

    lax.fori_loop(0, (filled + UNROLL - 1) // UNROLL, several, 0)
    return jnp.where(total[...] > 0.0, highest[...] + jnp.log2(total[...]), LOW)


def row_kernel(
    source_all, p0, p1, p2, p3, codes, counts, partial, late_all, source, late, early, highest, total, entries, sem
):
    load = pltpu.make_async_copy(source_all, source, sem.at[0])
    load.start()
    lane = iota((128, 128), 1)
    turned = indicator(((lane >= 100) & (lane <= 102)) | ((lane >= 105) & (lane <= 107)))
    sub8 = iota((8, 128), 0)
    for d, pack in enumerate((p0, p1, p2, p3)):

        def build(b):
            span = pl.ds(pl.multiple_of(b * 128, 128), 128)
            h, m, l = three(pack[0:32, span] * (KAPPA / 16.0))
            ah, am, al = three(jnp.broadcast_to(pack[32:33, span], (8, 128)))
            part = jnp.where(sub8 < 3, 1.0, jnp.where(sub8 == 3, ah, jnp.where(sub8 == 7, am, 0.0)))
            last = jnp.where(sub8 == 0, al, 0.0)
            rows = jnp.concatenate([h, m, l, part, last, jnp.zeros((16, 128), f32)], axis=0).astype(bf16).T
            place = pl.ds(pl.multiple_of(d * TGT + b * 128, 128), 128)
            early[place, :] = rows
            late[place, :] = rows + turned

        def several(g, carry):
            for u in range(16):
                build(g * 16 + u)
            return carry

        lax.fori_loop(0, TGT // 2048, several, 0)

    store = pltpu.make_async_copy(late, late_all, sem.at[1])
    store.start()
    load.wait()
    partial[...] = tiles(
        lambda s, t: early[pl.ds(pl.multiple_of(t * BLK, BLK), BLK), :],
        lambda s, t, half: source[pl.ds(pl.multiple_of(s * BLK + half * 128, 128), 128), :],
        lambda s, t: s,
        highest,
        total,
        counts,
        codes,
        entries,
    )
    store.wait()


def merged(parts):
    top = functools.reduce(jnp.maximum, parts)
    return top + jnp.log2(sum(jnp.exp2(part - top) for part in parts))


def merge_kernel(*refs):
    refs[-1][...] = merged([ref[...] for ref in refs[:-1]])


def col_kernel(source_all, late_all, lse, codes, counts, partial, filled, late, highest, total, entries, sems):
    share = CHUNK // LOADS
    second = pltpu.make_async_copy(late_all, late, sems.at[LOADS])
    loads = []
    for k in range(LOADS):
        here = slice(k * share, (k + 1) * share)
        loads.append(pltpu.make_async_copy(source_all.at[here, :], filled.at[here, :], sems.at[k]))
        loads[-1].start()
    second.start()
    sub8 = iota((8, 128), 0)

    def fill(g, carry):
        for u in range(FILL):
            row = -lse[pl.ds(g * FILL + u, 1), :]
            h, m, l = three(jnp.broadcast_to(row, (8, 128)))
            part = jnp.where(sub8 == 1, h, jnp.where(sub8 == 2, m, jnp.where(sub8 == 3, l, 0.0)))
            rows = jnp.concatenate([jnp.zeros((104, 128), f32), part, jnp.zeros((16, 128), f32)], axis=0)
            span = pl.ds(pl.multiple_of((g * FILL + u) * 128, 128), 128)
            filled[span, :] = filled[span, :] + rows.astype(bf16).T
        return carry

    for k in range(LOADS):
        loads[k].wait()
        lax.fori_loop(k * (share // 128 // FILL), (k + 1) * (share // 128 // FILL), fill, 0)
    second.wait()
    partial[...] = tiles(
        lambda s, t: filled[pl.ds(pl.multiple_of(s * BLK, BLK), BLK), :],
        lambda s, t, half: late[pl.ds(pl.multiple_of(t * BLK + half * 128, 128), 128), :],
        lambda s, t: t,
        highest,
        total,
        counts,
        codes,
        entries,
    )


def flat(block):
    return jnp.concatenate([block[u : u + 1, :] for u in range(8)], axis=1)


def spread(order_row, value_row, high_rows):
    n = order_row.shape[1]
    high = indicator(iota((high_rows, n), 0) == order_row // 128)
    match = iota((128, n), 0) == lax.rem(order_row, 128)
    first = value_row.astype(bf16).astype(f32)
    low = jnp.concatenate(
        [jnp.where(match, first, 0.0), jnp.where(match, value_row - first, 0.0)], axis=0
    ).astype(bf16)
    return lax.dot_general(high, low, NT, preferred_element_type=f32)


def scatter_kernel(mass, order, first_lse, second_lse, chunk, *refs):
    half = lax.rem(lax.axis_index("col") // Y, 2)
    out, total = refs[-2:]
    number = iota((256, 1024), 0).astype(f32).astype(bf16)
    one, zero = jnp.ones((), bf16), jnp.zeros((), bf16)
    if mass is None:
        total[...] = jnp.zeros(total.shape, f32)
    else:
        total[...] = refs[0][...]
    for k, lse in enumerate((first_lse, second_lse)):
        first = chunk[k] * (2 * NB)

        def product(g):
            cell = flat(order[pl.ds(pl.multiple_of(first + g * 8, 8), 8), :])
            value = flat(lse[pl.ds(pl.multiple_of(g * 8, 8), 8), :])
            column = lax.rem(cell // 128, 256).astype(f32).astype(bf16)
            row = ((cell // (SRC // 2) - half) * 128 + lax.rem(cell, 128)).astype(f32).astype(bf16)
            big = value.astype(bf16)
            small = (value - big.astype(f32)).astype(bf16)
            match = number[0:128] == row
            left = jnp.concatenate([jnp.where(match, big, zero), jnp.where(match, small, zero)], axis=0)
            right = jnp.where(number == column, one, zero)
            return lax.dot_general(left, right, NT, preferred_element_type=f32)

        def step(g, carry):
            total[...] += sum(product(g * SCATTER + u) for u in range(SCATTER))
            return carry

        lax.fori_loop(0, NB // 4 // SCATTER, step, 0)
    if mass is None:
        out[...] = total[...]
        return
    base = half * 256
    for side in range(2):
        here = slice(side * 128, side * 128 + 128)
        both = total[0:128, here] + total[128:256, here]
        weight = mass[pl.ds(pl.multiple_of(base + side * 128, 128), 128), :]
        out[here, :] = 0.1 * weight - (0.1 * LN2) * both.T


def last_scatter_kernel(mass, *refs):
    scatter_kernel(mass, *refs)


def final_kernel(*refs):
    order, mass, potential, own, other, source_out, out = refs[4:]
    half = lax.rem(lax.axis_index("col") // Y, 2)
    source_out[pl.ds(pl.multiple_of(half * 256, 256), 256), :] = own[...]
    source_out[pl.ds(pl.multiple_of(256 - half * 256, 256), 256), :] = other[...]
    lse = merged([ref[...] for ref in refs[:4]])
    total = jnp.zeros((TGT // 128, 256), f32)
    for g in range(TGT // 1024):
        total += spread(flat(order[g * 8 : g * 8 + 8, :]), flat(lse[g * 8 : g * 8 + 8, :]), TGT // 128)
    out[...] = 0.1 * mass[...] + potential[...] - (0.1 * LN2) * (total[:, 0:128] + total[:, 128:256])


def y_shift(d):
    return [(z * Y + y, z * Y + (y + d) % Y) for z in range(Z) for y in range(Y)]


def z_shift(d):
    return [(z * Y + y, (z + d) % Z * Y + y) for z in range(Z) for y in range(Y)]


def z_pair():
    return [(z * Y + y, (z ^ 1) * Y + y) for z in range(Z) for y in range(Y)]


def row_pair():
    return [(r, r ^ 1) for r in range(ROWS)]


def row_shift(d):
    return [(r, (r + d) % ROWS) for r in range(ROWS)]


def body(
    source_coords,
    target_coords,
    source_order,
    target_order,
    source_mass,
    target_mass,
    target_potential,
    tile_source,
    tile_target,
    tile_count,
):
    shape = jax.ShapeDtypeStruct
    y = lax.rem(lax.axis_index("col"), Y)
    mass = source_mass.reshape(SRC // 128, 128)

    pack = call(
        target_kernel,
        "target_gather",
        shape((PACK, TGT), f32),
        [anywhere()] * 5 + [smem()],
        [
            pltpu.VMEM((48, TGT), bf16),
            pltpu.VMEM((PC, TGT), bf16),
            pltpu.VMEM((1, TGT), jnp.int32),
            pltpu.VMEM((1, TGT), f32),
            pltpu.VMEM((1, CAP), jnp.int32),
            pltpu.VMEM((1, CAP), jnp.int32),
            pltpu.SemaphoreType.DMA((5,)),
        ],
        flops=2 * 48 * TGT * TGT,
        limit=60,
    )(
        target_coords,
        target_order,
        target_potential.reshape(1, TGT),
        tile_source.reshape(1, CAP),
        tile_target.reshape(1, CAP),
        tile_count,
    )
    packs = [pack] + [lax.ppermute(pack, "col", y_shift(d)) for d in range(1, Y)]

    source = call(
        gather_kernel,
        "source_gather",
        shape((CHUNK, 128), bf16),
        [anywhere()] * 3,
        [
            pltpu.VMEM((SRC, 128), f32),
            pltpu.VMEM((BLK, 128), f32),
            pltpu.VMEM((PC, SRC), bf16),
            pltpu.VMEM((SRC // 128, 128), f32),
            pltpu.SMEM((1, CHUNK), jnp.int32),
            pltpu.VMEM((CHUNK, 128), bf16),
            pltpu.SemaphoreType.DMA((LOADS,)),
            pltpu.SemaphoreType.DMA((2,)),
            pltpu.SemaphoreType.DMA((STORES,)),
        ],
        flops=2 * 10**10,
        nbytes=64 * 2**20,
        limit=56,
        out_specs=anywhere(),
    )(source_coords, mass, source_order)

    lists = jnp.concatenate([lax.dynamic_slice(p, (PACK - 1, y * CAP), (1, CAP)) for p in packs], axis=0)
    codes = lists.astype(jnp.int32) - 1
    counts = jnp.sum((lists > 0.5).astype(jnp.int32), axis=1)

    partial, late = call(
        row_kernel,
        "row_pass",
        [shape((2 * NB, 128), f32), shape((Y * TGT, 128), bf16)],
        [anywhere()] + [vmem()] * 4 + [smem()] * 2,
        [
            pltpu.VMEM((CHUNK, 128), bf16),
            pltpu.VMEM((Y * TGT, 128), bf16),
            pltpu.VMEM((Y * TGT, 128), bf16),
            pltpu.VMEM((2 * NB, 128), f32),
            pltpu.VMEM((2 * NB, 128), f32),
            pltpu.SMEM((Y * CAP,), jnp.int32),
            pltpu.SemaphoreType.DMA((2,)),
        ],
        out_specs=[vmem(), anywhere()],
    )(source, *packs, codes, counts)

    partials = [partial] + [lax.ppermute(partial, "col", z_shift(d)) for d in (2, 4, 6)]
    lse = call(merge_kernel, "row_merge_four", shape((2 * NB, 128), f32), [vmem()] * 4, [])(*partials)
    partials = [lse, lax.ppermute(lse, "col", z_pair())]
    lse = call(merge_kernel, "row_merge_two", shape((2 * NB, 128), f32), [vmem()] * 2, [])(*partials)
    lses = [lse] + [lax.ppermute(lse, "col", y_shift(d)) for d in range(1, Y)]

    target_partial = call(
        col_kernel,
        "col_pass",
        shape((2 * Y * TB, 128), f32),
        [anywhere(), anywhere(), vmem()] + [smem()] * 2,
        [
            pltpu.VMEM((CHUNK, 128), bf16),
            pltpu.VMEM((Y * TGT, 128), bf16),
            pltpu.VMEM((2 * Y * TB, 128), f32),
            pltpu.VMEM((2 * Y * TB, 128), f32),
            pltpu.SMEM((Y * CAP,), jnp.int32),
            pltpu.SemaphoreType.DMA((LOADS + 1,)),
        ],
        flops=2 * 10**10,
        exps=10**7,
    )(source, late, lse, codes, counts)

    order_rows = source_order.reshape(SRC // 128, 128)
    cost = dict(flops=2 * 512 * 256 * CHUNK, nbytes=2**20)
    keep = [pltpu.VMEM((256, 256), f32)]
    chunks = lax.rem(y + Y - jnp.arange(Y, dtype=jnp.int32), Y)

    def merge(name, parts):
        return call(merge_kernel, name, shape((2 * TB, 128), f32), [vmem()] * len(parts), [])(*parts)

    own = [target_partial[0 : 2 * TB]] + [
        lax.ppermute(target_partial[2 * d * TB : 2 * (d + 1) * TB], "col", y_shift(-d)) for d in range(1, Y)
    ]
    scattered = call(
        functools.partial(scatter_kernel, None),
        "source_scatter_0",
        shape((256, 256), f32),
        [vmem()] * 3 + [smem()],
        keep,
        **cost,
    )(order_rows, lses[0], lses[1], chunks[0:2])
    own, scattered = lax.optimization_barrier((own, scattered))
    own = merge("col_merge_y", own)
    own = [own, lax.ppermute(own, "row", row_pair())]
    mine = call(
        last_scatter_kernel,
        "source_scatter_1",
        shape((SRC // 256, 128), f32),
        [vmem()] * 4 + [smem(), vmem()],
        keep,
        **cost,
    )(mass, order_rows, lses[2], lses[3], chunks[2:4], scattered)
    own, mine = lax.optimization_barrier((own, mine))
    other = lax.ppermute(mine, "col", z_pair())
    own = merge("col_merge_core", own)
    own = [own] + [lax.ppermute(own, "row", row_shift(d)) for d in (2, 4, 6)]
    source_update, target_update = call(
        final_kernel,
        "target_scatter",
        [shape((SRC // 128, 128), f32), shape((TGT // 128, 128), f32)],
        [vmem()] * 9,
        [],
    )(
        *own,
        target_order.reshape(TGT // 128, 128),
        target_mass.reshape(TGT // 128, 128),
        target_potential.reshape(TGT // 128, 128),
        mine,
        other,
    )
    return (source_update.reshape(SRC), target_update.reshape(TGT))


def solution(mesh):
    in_specs = (
        P(None, "row"),
        P(None, "col"),
        P("row", None),
        P("col", None),
        P("row"),
        P("col"),
        P("col"),
        P("row", "col", None),
        P("row", "col", None),
        P("row", "col"),
    )
    out_specs = (P("row"), P("col"))
    return jax.shard_map(body, mesh=mesh, in_specs=in_specs, out_specs=out_specs, check_vma=False)
```
